32 devices in a mesh: groups: 2 (over x), adapter: 16 (over z, y, core).
Axes of the slice: x: 2, y: 2, z: 4, core: 2. Of those that a mesh axis runs over, the one named last changes fastest.
Arguments:
- queries: bfloat16 [512, 4096], P(('groups', 'adapter')), parts along dimension 0, may hold values from -4.5 to 4.5
- key_cache: bfloat16 [512, 160, 512], P(('groups', 'adapter')), parts along dimension 0, may hold values from -4.5 to 4.5
- value_cache: bfloat16 [512, 160, 512], P(('groups', 'adapter')), parts along dimension 0, may hold values from -4.5 to 4.5
- lengths: int32 [512], P(('groups', 'adapter')), parts along dimension 0, may hold values from 2 to 160, as said below
- adapter_ids: int32 [512], P(('groups', 'adapter')), parts along dimension 0, may hold values from 0 to 511, as said below
- output_weight_rows: bfloat16 [4096, 8192], P(None, 'adapter'), may hold values from -0.09375 to 0.09375
- basis_in: bfloat16 [4096, 256], replicated, may hold values from -0.09375 to 0.09375
- shared_output_basis: bfloat16 [8192, 256], P('adapter'), may hold values from -0.375 to 0.375
- coefficients: bfloat16 [512, 256, 256], P('adapter'), may hold values from -0.375 to 0.375
Outputs:
- output: bfloat16 [512, 8192], P('groups', 'adapter'), parts along dimension 0
The draws below stay inside these ranges and needn't reach their ends.
There are 2 independent parts, one for each index of `groups`. The reference program is written for one: setup_inputs(seed, part) draws one part's arguments, and reference() takes and returns one part's arrays. A program takes and returns all parts, laid end to end along the dimension named above; an argument that names none is the same for every part. Nothing has to cross between parts.
Inputs may be any that keep to these rules, and one draw needn't show every extreme that they name: `lengths`: every request has at least two positions in use; in every group some request has exactly 160. `adapter_ids`: within a group at most 32 requests have ids in one block of ids b * 32 to (b + 1) * 32 - 1, and some block has exactly 32.
All inputs are finite; a program needn't handle non-finite values.
Results may differ from the reference program's by a relative error of at most 0.014.
Values may be sent and summed in bfloat16 or wider, within the bound.
A program may use at most 64 MiB of HBM per device.

```python
import jax
import jax.numpy as jnp
from jax import lax

D = 8192
HEAD_DIM = 128
Q_HEADS = 32
KV_HEADS = 4
RANK = 256
ADP_DEV = 32
REQ_DEV = 16
CTX = 160
REQUESTS = 256
ADAPTERS = 512
CAP = 32


def draw_queries(key, part):
    key = jax.random.fold_in(key, 1)
    shape = (REQUESTS, KV_HEADS, Q_HEADS // KV_HEADS, HEAD_DIM)
    drawn_draw = jnp.clip(jax.random.normal(key, shape, jnp.float32), -4.5, 4.5)
    return drawn_draw.reshape(REQUESTS, Q_HEADS * HEAD_DIM).astype(jnp.bfloat16)


def draw_key_cache(key, part):
    key = jax.random.fold_in(key, 2)
    shape = (REQUESTS, CTX, KV_HEADS, HEAD_DIM)
    drawn_draw = jnp.clip(jax.random.normal(key, shape, jnp.float32), -4.5, 4.5)
    return drawn_draw.reshape(REQUESTS, CTX, KV_HEADS * HEAD_DIM).astype(jnp.bfloat16)


def draw_lengths(key, part):
    key = jax.random.fold_in(key, 3)
    drawn_len = jax.random.randint(key, (REQUESTS,), 2, CTX + 1)
    top_row = jax.random.randint(jax.random.fold_in(key, 1), (), 0, REQUESTS)
    return jnp.where(jnp.arange(REQUESTS) == top_row, CTX, drawn_len).astype(jnp.int32)


def draw_adapter_ids(key, part):
    key = jax.random.fold_in(key, 4)
    owners = ADAPTERS // ADP_DEV
    slot_count = owners * CAP
    order_key, popular_adapter_key, shuffle_key, local_key = jax.random.split(key, 4)
    slot_score = jax.random.permutation(order_key, slot_count).astype(jnp.int32)
    hot_owner = jax.random.randint(popular_adapter_key, (), 0, owners)
    slot_index = jnp.arange(slot_count, dtype=jnp.int32)
    slot_score = jnp.where(slot_index // CAP == hot_owner, -1 - slot_index % CAP, slot_score)
    picked = jnp.argsort(slot_score, stable=True)[:REQUESTS]
    picked = picked[jax.random.permutation(shuffle_key, REQUESTS)]
    local_ids = jax.random.randint(local_key, (REQUESTS,), 0, ADP_DEV)
    return (picked // CAP * ADP_DEV + local_ids).astype(jnp.int32)


def shard_levels(rng, shape, cuts, low, top_value):
    def one(dim, parts):
        steps = jax.random.uniform(jax.random.fold_in(jax.random.fold_in(rng, 6), dim), (parts,), jnp.float32, low / len(cuts), top_value / len(cuts))
        return jnp.repeat(jnp.exp(steps), shape[dim] // parts).reshape((-1,) + (1,) * (len(shape) - dim - 1))

    gain = one(*cuts[0])
    for cut in cuts[1:]:
        gain = gain * one(*cut)
    return gain


def gaussian(stream_key, extent, deviation, bound, shards=(), held_as=jnp.bfloat16):
    entries = jax.random.normal(stream_key, extent, jnp.float32) * deviation
    if len(shards) > 0:
        entries = shard_levels(stream_key, extent, shards, -0.22, 0.18) * entries
    return jnp.clip(entries, min=-bound, max=bound).astype(held_as)


def setup_inputs(seed: int = 0, part: int = 0) -> dict:
    seeds = jax.random.split(jax.random.key(seed), 10)
    part_splits = jax.random.split(jax.random.fold_in(seeds[9], part), 10)
    return {
        "queries": draw_queries(jax.random.fold_in(jax.random.fold_in(seeds[9], part), 71), part),
        "key_cache": draw_key_cache(jax.random.fold_in(jax.random.fold_in(seeds[9], part), 71), part),
        "value_cache": gaussian(part_splits[2], (REQUESTS, CTX, KV_HEADS * HEAD_DIM), 1.0, 4.5, ((0, 16),)),
        "lengths": draw_lengths(jax.random.fold_in(jax.random.fold_in(seeds[9], part), 71), part),
        "adapter_ids": draw_adapter_ids(jax.random.fold_in(jax.random.fold_in(seeds[9], part), 71), part),
        "output_weight_rows": gaussian(seeds[5], (Q_HEADS * HEAD_DIM, D), (Q_HEADS * HEAD_DIM) ** -0.5, 0.09375, ((1, 16),)),
        "basis_in": gaussian(seeds[6], (Q_HEADS * HEAD_DIM, RANK), (Q_HEADS * HEAD_DIM) ** -0.5, 0.09375),
        "shared_output_basis": gaussian(seeds[7], (D, RANK), RANK ** -0.5, 0.375, ((0, 16),)),
        "coefficients": gaussian(seeds[8], (ADAPTERS, RANK, RANK), RANK ** -0.5, 0.375, ((0, 16),)),
    }


def attend(queries, key_cache, value_cache, lengths):
    req_count = queries.shape[0]
    group_size = Q_HEADS // KV_HEADS
    query_f32 = queries.astype(jnp.float32).reshape(req_count, KV_HEADS, group_size, HEAD_DIM)
    key_f32 = key_cache.astype(jnp.float32).reshape(req_count, CTX, KV_HEADS, HEAD_DIM)
    value_f32 = value_cache.astype(jnp.float32).reshape(req_count, CTX, KV_HEADS, HEAD_DIM)
    scores = jnp.einsum("rkgd,rtkd->rkgt", query_f32, key_f32) * (HEAD_DIM ** -0.5)
    valid_mask = (jnp.arange(CTX, dtype=jnp.int32)[None, :] < lengths[:, None])[:, None, None, :]
    scores = jnp.where(valid_mask, scores, -1e30)
    row_max = jnp.max(scores, axis=-1, keepdims=True)
    exp_terms = jnp.where(valid_mask, jnp.exp(scores - row_max), 0.0)
    prob_weights = (exp_terms / jnp.sum(exp_terms, axis=-1, keepdims=True)).astype(jnp.bfloat16)
    attended = jnp.einsum("rkgt,rtkd->rkgd", prob_weights.astype(jnp.float32), value_f32)
    return attended.reshape(req_count, Q_HEADS * HEAD_DIM).astype(jnp.bfloat16)


def reference(queries, key_cache, value_cache, lengths, adapter_ids, output_weight_rows, basis_in, shared_output_basis, coefficients):
    attended = attend(queries, key_cache, value_cache, lengths)
    projected = jnp.dot(attended, basis_in, preferred_element_type=jnp.float32).astype(jnp.bfloat16)

    def apply_block(inputs):
        block_rows, block_ids = inputs
        chosen_coef = coefficients[block_ids].astype(jnp.float32)
        return jnp.einsum("rk,rkj->rj", block_rows.astype(jnp.float32), chosen_coef).astype(jnp.bfloat16)

    blocks = REQUESTS // REQ_DEV
    adapter_applied = lax.map(apply_block, (projected.reshape(blocks, REQ_DEV, RANK), adapter_ids.reshape(blocks, REQ_DEV)))
    adapter_applied = adapter_applied.reshape(REQUESTS, RANK)
    base_contribution = jnp.dot(attended, output_weight_rows, preferred_element_type=jnp.float32)
    low_rank_contribution = jnp.dot(adapter_applied, shared_output_basis.T, preferred_element_type=jnp.float32)
    return (base_contribution + low_rank_contribution).astype(jnp.bfloat16)
```

```python
import functools

import jax
import jax.numpy as jnp
from jax import lax
from jax.experimental import pallas as pl
from jax.experimental.pallas import tpu as pltpu
from jax.sharding import PartitionSpec as P

HEAD_DIM = 128
Q_HEADS = 32
KV_HEADS = 4
CAP = 32
PAIRS = KV_HEADS // 2
GROUP = Q_HEADS // KV_HEADS
F32 = jnp.float32
BF16 = jnp.bfloat16


def kernel(
    zs,
    ys,
    lengths,
    ids,
    q_hbm,
    k_hbm,
    v_hbm,
    w_hbm,
    basis_hbm,
    sob_hbm,
    coef_hbm,
    out_ref,
    q_buf,
    k_buf,
    v_buf,
    w_buf,
    basis_buf,
    sob_buf,
    coef_buf,
    q32,
    a32,
    att_all,
    proj_all,
    res_all,
    acc,
    local_sem,
    send_sem,
    recv_sem,
):
    n = zs * ys * 2
    me = lax.axis_index("adapter")
    core = lax.rem(me, 2)
    y = lax.rem(lax.div(me, 2), ys)
    z = lax.div(me, 2 * ys)

    def dev(zz, yy, cc):
        return (zz * ys + yy) * 2 + cc

    z_at = [lax.rem(z + step, zs) for step in range(zs)]
    z_peers = [dev(z_at[step], y, core) for step in range(1, zs)]
    y_peer = dev(z, 1 - y, core) if ys == 2 else None
    sibling = dev(z, y, 1 - core)
    partners = z_peers + ([y_peer] if ys == 2 else []) + [sibling]

    reqs, ctx = k_hbm.shape[0], k_hbm.shape[1]
    copies = {}

    def fetch(name, src, dst):
        copies[name] = pltpu.make_async_copy(src, dst, local_sem.at[len(copies)])
        copies[name].start()

    fetch("q", q_hbm, q_buf)
    for p in range(PAIRS):
        cols = pl.ds(p * 2 * HEAD_DIM, 2 * HEAD_DIM)
        fetch(("k", p), k_hbm.at[:, :, cols], k_buf.at[p])
        fetch(("v", p), v_hbm.at[:, :, cols], v_buf.at[p])
    fetch("basis", basis_hbm, basis_buf)
    fetch("coef", coef_hbm, coef_buf)
    fetch("w", w_hbm, w_buf)
    fetch("sob", sob_hbm, sob_buf)

    barrier = pltpu.get_barrier_semaphore()
    for partner in partners:
        pl.semaphore_signal(
            barrier, inc=1, device_id={"adapter": partner}, device_id_type=pl.DeviceIdType.MESH
        )

    payloads = [att_all.at[j] for j in range(KV_HEADS)] + [proj_all, res_all]
    sends = [[] for _ in payloads]

    def send(c, origin, target):
        ref = payloads[c].at[origin]
        copy = pltpu.make_async_remote_copy(
            src_ref=ref,
            dst_ref=ref,
            send_sem=send_sem.at[c, len(sends[c])],
            recv_sem=recv_sem.at[c, origin],
            device_id={"adapter": target},
            device_id_type=pl.DeviceIdType.MESH,
        )
        copy.start()
        sends[c].append(copy)

    def arrive(c, origin):
        ref = payloads[c].at[origin]
        pltpu.make_async_copy(ref, ref, recv_sem.at[c, origin]).wait()

    def stage_own(c):
        for peer in z_peers:
            send(c, me, peer)
        if ys == 2:
            send(c, me, y_peer)
        send(c, me, sibling)

    def stage_z(c):
        for step in range(1, zs):
            origin = dev(z_at[step], y, core)
            arrive(c, origin)
            if ys == 2:
                send(c, origin, y_peer)
            send(c, origin, sibling)

    def stage_y(c):
        if ys == 2:
            for step in range(zs):
                origin = dev(z_at[step], 1 - y, core)
                arrive(c, origin)
                send(c, origin, sibling)

    def stage_core(c):
        for step in range(zs):
            arrive(c, dev(z_at[step], y, 1 - core))
        if ys == 2:
            for step in range(zs):
                arrive(c, dev(z_at[step], 1 - y, 1 - core))

    zero = jnp.zeros((reqs, GROUP, HEAD_DIM), F32)
    copies["q"].wait()
    for p in range(PAIRS):
        q32[p, :, :GROUP, HEAD_DIM:] = zero
        q32[p, :, GROUP:, :HEAD_DIM] = zero
        for h in range(2 * GROUP):
            g = p * 2 * GROUP + h
            lo = (h // GROUP) * HEAD_DIM
            q32[p, :, h, lo : lo + HEAD_DIM] = q_buf[:, g * HEAD_DIM : (g + 1) * HEAD_DIM].astype(F32)
    used = jnp.stack(
        [jnp.full((2 * GROUP, ctx), lengths[r], jnp.int32) for r in range(reqs)]
    )
    valid = lax.broadcasted_iota(jnp.int32, (reqs, 2 * GROUP, ctx), 2) < used

    def attend(p):
        copies[("k", p)].wait()
        scores = jnp.einsum(
            "rhd,rtd->rht", q32[p].astype(BF16), k_buf[p], preferred_element_type=F32
        ) * HEAD_DIM ** (-0.5)
        scores = jnp.where(valid, scores, -1e30)
        row_max = jnp.max(scores, axis=-1, keepdims=True)
        terms = jnp.where(valid, jnp.exp(scores - row_max), 0.0)
        probs = (terms / jnp.sum(terms, axis=-1, keepdims=True)).astype(BF16)
        copies[("v", p)].wait()
        att = jnp.einsum("rht,rtd->rhd", probs, v_buf[p], preferred_element_type=F32)
        a32[p, :, :GROUP, :] = att[:, :GROUP, :HEAD_DIM]
        a32[p, :, GROUP:, :] = att[:, GROUP:, HEAD_DIM:]
        for h in range(2 * GROUP):
            lo = (h % GROUP) * HEAD_DIM
            att_all[2 * p + h // GROUP, me, :, lo : lo + HEAD_DIM] = a32[p, :, h, :].astype(BF16)

    attend(0)
    pl.semaphore_wait(barrier, len(partners))
    stage_own(0)
    stage_own(1)
    attend(1)

    copies["basis"].wait()
    wide = GROUP * HEAD_DIM
    projected = jnp.zeros((reqs, basis_buf.shape[1]), F32)
    for j in range(KV_HEADS):
        projected += jnp.dot(
            att_all[j, me], basis_buf[j * wide : (j + 1) * wide, :], preferred_element_type=F32
        )
    rank = basis_buf.shape[1]
    per_owner = coef_buf.shape[0]
    row_id = lax.broadcasted_iota(jnp.int32, (reqs, HEAD_DIM), 0)
    left = lax.broadcasted_iota(jnp.int32, (reqs, HEAD_DIM), 1) < HEAD_DIM // 2
    id_cols = jnp.zeros((reqs, HEAD_DIM), jnp.int32)
    for r in range(reqs):
        block = lax.div(ids[r], per_owner)
        both = jnp.where(left, block, ids[r] - block * per_owner)
        id_cols = jnp.where(row_id == r, both, id_cols)
    proj_all[me, :, :rank] = projected.astype(BF16)
    proj_all[me, :, rank:] = id_cols.astype(F32).astype(BF16)
    PROJ, RES = KV_HEADS, KV_HEADS + 1
    stage_own(PROJ)
    stage_own(2)
    stage_own(3)

    stage_z(0)
    stage_z(1)
    stage_z(PROJ)
    stage_y(0)
    stage_y(1)
    stage_y(PROJ)
    stage_core(PROJ)

    total = n * reqs
    rows = proj_all[:, :, :rank].reshape(total, rank)
    id_all = proj_all[:, :, rank:].reshape(total, HEAD_DIM)
    half = HEAD_DIM // 2
    owner_col = id_all.astype(F32)[:, :1]
    take = (lax.broadcasted_iota(jnp.int32, (16, HEAD_DIM), 1) == 0).astype(F32).astype(BF16)
    owner_row = lax.dot_general(
        take, id_all, (((1,), (1,)), ((), ())), preferred_element_type=F32
    )[:1, :]
    same = owner_col == owner_row
    r_row = lax.broadcasted_iota(jnp.int32, (total, total), 0)
    r_col = lax.broadcasted_iota(jnp.int32, (total, total), 1)
    slot_row = jnp.sum(jnp.where(same & (r_row < r_col), 1.0, 0.0), axis=0, keepdims=True)
    slot_col = jnp.sum(jnp.where(same & (r_col < r_row), 1.0, 0.0), axis=1, keepdims=True)

    slot_list = lax.broadcasted_iota(jnp.int32, (CAP, total), 0).astype(F32)
    picks = jnp.where(
        (owner_row == me.astype(F32)) & (slot_row == slot_list), 1.0, 0.0
    ).astype(BF16)
    bucket = jnp.dot(picks, rows, preferred_element_type=F32)
    local = jnp.dot(picks, id_all, preferred_element_type=F32)[:, half : half + 1]
    copies["coef"].wait()
    spread = jnp.concatenate(
        [jnp.where(local == float(a), bucket, 0.0).astype(BF16) for a in range(per_owner)], axis=1
    )
    result = jnp.dot(
        spread, coef_buf[...].reshape(per_owner * rank, rank), preferred_element_type=F32
    )
    res_all[me] = result.astype(BF16)
    stage_own(RES)

    copies["w"].wait()

    def base(j):
        return jnp.dot(
            att_all[j].reshape(total, wide),
            w_buf[j * wide : (j + 1) * wide, :],
            preferred_element_type=F32,
        )

    stage_z(2)
    stage_z(3)
    stage_z(RES)
    stage_core(0)
    acc[...] = base(0)
    stage_y(2)
    stage_y(3)
    stage_y(RES)
    stage_core(1)
    acc[...] += base(1)
    stage_core(2)
    acc[...] += base(2)
    stage_core(RES)
    place = jnp.where(
        lax.broadcasted_iota(jnp.int32, (total, n * CAP), 1).astype(F32)
        == owner_col * CAP + slot_col,
        1.0,
        0.0,
    ).astype(BF16)
    adapted = jnp.dot(
        place, res_all[...].reshape(n * CAP, rank), preferred_element_type=F32
    ).astype(BF16)
    copies["sob"].wait()
    acc[...] += lax.dot_general(
        adapted, sob_buf[...], (((1,), (1,)), ((), ())), preferred_element_type=F32
    )
    stage_core(3)
    out_ref[...] = (acc[...] + base(3)).astype(out_ref.dtype)

    for c in range(len(payloads)):
        for copy in sends[c]:
            copy.wait_send()


def on_device(zs, ys, queries, key_cache, value_cache, lengths, ids, w, basis, sob, coef):
    n = zs * ys * 2
    reqs, ctx = key_cache.shape[:2]
    rank = basis.shape[1]
    wide = GROUP * HEAD_DIM
    smem = pl.BlockSpec(memory_space=pltpu.SMEM)
    hbm = pl.BlockSpec(memory_space=pl.ANY)
    vmem = pl.BlockSpec(memory_space=pltpu.VMEM)
    fetches = 5 + 2 * PAIRS
    return pl.pallas_call(
        functools.partial(kernel, zs, ys),
        out_shape=jax.ShapeDtypeStruct((n * reqs, w.shape[1]), BF16),
        in_specs=[smem, smem] + [hbm] * 7,
        out_specs=vmem,
        scratch_shapes=[
            pltpu.VMEM(queries.shape, BF16),
            pltpu.VMEM((PAIRS, reqs, ctx, 2 * HEAD_DIM), BF16),
            pltpu.VMEM((PAIRS, reqs, ctx, 2 * HEAD_DIM), BF16),
            pltpu.VMEM(w.shape, BF16),
            pltpu.VMEM(basis.shape, BF16),
            pltpu.VMEM(sob.shape, BF16),
            pltpu.VMEM(coef.shape, BF16),
            pltpu.VMEM((PAIRS, reqs, 2 * GROUP, 2 * HEAD_DIM), F32),
            pltpu.VMEM((PAIRS, reqs, 2 * GROUP, HEAD_DIM), F32),
            pltpu.VMEM((KV_HEADS, n, reqs, wide), BF16),
            pltpu.VMEM((n, reqs, rank + HEAD_DIM), BF16),
            pltpu.VMEM((n, CAP, rank), BF16),
            pltpu.VMEM((n * reqs, w.shape[1]), F32),
            pltpu.SemaphoreType.DMA((fetches,)),
            pltpu.SemaphoreType.DMA((KV_HEADS + 2, n)),
            pltpu.SemaphoreType.DMA((KV_HEADS + 2, n)),
        ],
        compiler_params=pltpu.CompilerParams(
            collective_id=0, has_side_effects=True, vmem_limit_bytes=58 * 1024 * 1024
        ),
    )(lengths, ids, queries, key_cache, value_cache, w, basis, sob, coef)


def solution(mesh):
    n = mesh.shape["adapter"]
    zs, ys = (4, 2) if n == 16 else (n // 2, 1)
    return jax.shard_map(
        functools.partial(on_device, zs, ys),
        mesh=mesh,
        in_specs=(
            P(("groups", "adapter"), None),
            P(("groups", "adapter"), None, None),
            P(("groups", "adapter"), None, None),
            P(("groups", "adapter")),
            P(("groups", "adapter")),
            P(None, "adapter"),
            P(),
            P("adapter", None),
            P("adapter", None, None),
        ),
        out_specs=P("groups", "adapter"),
        check_vma=False,
    )
```

```python
import functools

import jax
import jax.numpy as jnp
from jax import lax
from jax.experimental import pallas as pl
from jax.experimental.pallas import tpu as pltpu
from jax.sharding import PartitionSpec as P

HEAD_DIM = 128
Q_HEADS = 32
KV_HEADS = 4
CAP = 32
PAIRS = KV_HEADS // 2
GROUP = Q_HEADS // KV_HEADS
F32 = jnp.float32
BF16 = jnp.bfloat16


def kernel(
    zs,
    ys,
    lengths,
    ids,
    q_hbm,
    k_hbm,
    v_hbm,
    w_hbm,
    basis_hbm,
    sob_hbm,
    coef_hbm,
    out_ref,
    q_buf,
    k_buf,
    v_buf,
    w_buf,
    basis_buf,
    sob_buf,
    coef_buf,
    q32,
    a32,
    att_all,
    proj_all,
    res_all,
    ids_all,
    acc,
    local_sem,
    send_sem,
    recv_sem,
):
    n = zs * ys * 2
    me = lax.axis_index("adapter")
    core = lax.rem(me, 2)
    y = lax.rem(lax.div(me, 2), ys)
    z = lax.div(me, 2 * ys)

    def dev(zz, yy, cc):
        return (zz * ys + yy) * 2 + cc

    z_at = [lax.rem(z + step, zs) for step in range(zs)]
    z_peers = [dev(z_at[step], y, core) for step in range(1, zs)]
    y_peer = dev(z, 1 - y, core) if ys == 2 else None
    sibling = dev(z, y, 1 - core)
    partners = z_peers + ([y_peer] if ys == 2 else []) + [sibling]

    reqs, ctx = k_hbm.shape[0], k_hbm.shape[1]
    copies = {}

    def fetch(name, src, dst):
        copies[name] = pltpu.make_async_copy(src, dst, local_sem.at[len(copies)])
        copies[name].start()

    fetch("q", q_hbm, q_buf)
    for p in range(PAIRS):
        cols = pl.ds(p * 2 * HEAD_DIM, 2 * HEAD_DIM)
        fetch(("k", p), k_hbm.at[:, :, cols], k_buf.at[p])
        fetch(("v", p), v_hbm.at[:, :, cols], v_buf.at[p])
    fetch("basis", basis_hbm, basis_buf)
    fetch("coef", coef_hbm, coef_buf)
    fetch("w", w_hbm, w_buf)
    fetch("sob", sob_hbm, sob_buf)

    barrier = pltpu.get_barrier_semaphore()
    for partner in partners:
        pl.semaphore_signal(
            barrier, inc=1, device_id={"adapter": partner}, device_id_type=pl.DeviceIdType.MESH
        )

    PROJ, RES, IDS = KV_HEADS, KV_HEADS + 1, KV_HEADS + 2
    payloads = [att_all.at[j] for j in range(KV_HEADS)] + [proj_all, res_all, ids_all]
    sends = [[] for _ in payloads]

    def send(c, origin, target):
        ref = payloads[c].at[origin]
        copy = pltpu.make_async_remote_copy(
            src_ref=ref,
            dst_ref=ref,
            send_sem=send_sem.at[c, len(sends[c])],
            recv_sem=recv_sem.at[c, origin],
            device_id={"adapter": target},
            device_id_type=pl.DeviceIdType.MESH,
        )
        copy.start()
        sends[c].append(copy)

    def arrive(c, origin):
        ref = payloads[c].at[origin]
        pltpu.make_async_copy(ref, ref, recv_sem.at[c, origin]).wait()

    def stage_own(c):
        for peer in z_peers:
            send(c, me, peer)
        if ys == 2:
            send(c, me, y_peer)
        send(c, me, sibling)

    def stage_z(c):
        for step in range(1, zs):
            origin = dev(z_at[step], y, core)
            arrive(c, origin)
            if ys == 2:
                send(c, origin, y_peer)
            send(c, origin, sibling)

    def stage_y(c):
        if ys == 2:
            for step in range(zs):
                origin = dev(z_at[step], 1 - y, core)
                arrive(c, origin)
                send(c, origin, sibling)

    def stage_core(c):
        for step in range(zs):
            arrive(c, dev(z_at[step], y, 1 - core))
        if ys == 2:
            for step in range(zs):
                arrive(c, dev(z_at[step], 1 - y, 1 - core))

    rank = basis_buf.shape[1]
    per_owner = coef_buf.shape[0]
    row_id = lax.broadcasted_iota(jnp.int32, (reqs, HEAD_DIM), 0)
    left = lax.broadcasted_iota(jnp.int32, (reqs, HEAD_DIM), 1) < HEAD_DIM // 2
    id_cols = jnp.zeros((reqs, HEAD_DIM), jnp.int32)
    for r in range(reqs):
        block = lax.div(ids[r], per_owner)
        both = jnp.where(left, block, ids[r] - block * per_owner)
        id_cols = jnp.where(row_id == r, both, id_cols)
    ids_all[me] = id_cols.astype(F32).astype(BF16)

    zero = jnp.zeros((reqs, GROUP, HEAD_DIM), F32)
    copies["q"].wait()
    for p in range(PAIRS):
        q32[p, :, :GROUP, HEAD_DIM:] = zero
        q32[p, :, GROUP:, :HEAD_DIM] = zero
        for h in range(2 * GROUP):
            g = p * 2 * GROUP + h
            lo = (h // GROUP) * HEAD_DIM
            q32[p, :, h, lo : lo + HEAD_DIM] = q_buf[:, g * HEAD_DIM : (g + 1) * HEAD_DIM].astype(F32)
    used = jnp.stack(
        [jnp.full((2 * GROUP, ctx), lengths[r], jnp.int32) for r in range(reqs)]
    )
    valid = lax.broadcasted_iota(jnp.int32, (reqs, 2 * GROUP, ctx), 2) < used

    def attend(p):
        copies[("k", p)].wait()
        scores = jnp.einsum(
            "rhd,rtd->rht", q32[p].astype(BF16), k_buf[p], preferred_element_type=F32
        ) * HEAD_DIM ** (-0.5)
        scores = jnp.where(valid, scores, -1e30)
        row_max = jnp.max(scores, axis=-1, keepdims=True)
        terms = jnp.where(valid, jnp.exp(scores - row_max), 0.0)
        probs = (terms / jnp.sum(terms, axis=-1, keepdims=True)).astype(BF16)
        copies[("v", p)].wait()
        att = jnp.einsum("rht,rtd->rhd", probs, v_buf[p], preferred_element_type=F32)
        a32[p, :, :GROUP, :] = att[:, :GROUP, :HEAD_DIM]
        a32[p, :, GROUP:, :] = att[:, GROUP:, HEAD_DIM:]
        for h in range(2 * GROUP):
            lo = (h % GROUP) * HEAD_DIM
            att_all[2 * p + h // GROUP, me, :, lo : lo + HEAD_DIM] = a32[p, :, h, :].astype(BF16)

    pl.semaphore_wait(barrier, len(partners))
    stage_own(IDS)
    attend(0)
    stage_own(0)
    stage_own(1)
    stage_z(IDS)
    attend(1)
    stage_y(IDS)

    copies["basis"].wait()
    wide = GROUP * HEAD_DIM
    projected = jnp.zeros((reqs, basis_buf.shape[1]), F32)
    for j in range(KV_HEADS):
        projected += jnp.dot(
            att_all[j, me], basis_buf[j * wide : (j + 1) * wide, :], preferred_element_type=F32
        )
    proj_all[me] = projected.astype(BF16)
    stage_own(PROJ)
    stage_own(2)
    stage_own(3)
    stage_core(IDS)

    total = n * reqs
    id_all = ids_all[...].reshape(total, HEAD_DIM)
    half = HEAD_DIM // 2
    owner_col = id_all.astype(F32)[:, :1]
    take = (lax.broadcasted_iota(jnp.int32, (16, HEAD_DIM), 1) == 0).astype(F32).astype(BF16)
    owner_row = lax.dot_general(
        take, id_all, (((1,), (1,)), ((), ())), preferred_element_type=F32
    )[:1, :]
    same = owner_col == owner_row
    r_row = lax.broadcasted_iota(jnp.int32, (total, total), 0)
    r_col = lax.broadcasted_iota(jnp.int32, (total, total), 1)
    slot_row = jnp.sum(jnp.where(same & (r_row < r_col), 1.0, 0.0), axis=0, keepdims=True)
    slot_col = jnp.sum(jnp.where(same & (r_col < r_row), 1.0, 0.0), axis=1, keepdims=True)

    slot_list = lax.broadcasted_iota(jnp.int32, (CAP, total), 0).astype(F32)
    picks = jnp.where(
        (owner_row == me.astype(F32)) & (slot_row == slot_list), 1.0, 0.0
    ).astype(BF16)
    local = jnp.dot(picks, id_all, preferred_element_type=F32)[:, half : half + 1]

    stage_z(0)
    stage_z(PROJ)
    stage_z(1)
    stage_y(0)
    stage_y(PROJ)
    stage_z(2)
    stage_core(PROJ)

    bucket = jnp.dot(
        picks, proj_all[...].reshape(total, rank), preferred_element_type=F32
    )
    copies["coef"].wait()
    spread = jnp.concatenate(
        [jnp.where(local == float(a), bucket, 0.0).astype(BF16) for a in range(per_owner)], axis=1
    )
    result = jnp.dot(
        spread, coef_buf[...].reshape(per_owner * rank, rank), preferred_element_type=F32
    )
    res_all[me] = result.astype(BF16)
    stage_own(RES)
    stage_z(3)
    stage_y(1)

    copies["w"].wait()

    def base(j):
        return jnp.dot(
            att_all[j].reshape(total, wide),
            w_buf[j * wide : (j + 1) * wide, :],
            preferred_element_type=F32,
        )

    stage_core(0)
    acc[...] = base(0)
    stage_y(2)
    stage_z(RES)
    stage_core(1)
    acc[...] += base(1)
    stage_y(3)
    stage_core(2)
    acc[...] += base(2)
    stage_y(RES)
    stage_core(RES)
    place = jnp.where(
        lax.broadcasted_iota(jnp.int32, (total, n * CAP), 1).astype(F32)
        == owner_col * CAP + slot_col,
        1.0,
        0.0,
    ).astype(BF16)
    adapted = jnp.dot(
        place, res_all[...].reshape(n * CAP, rank), preferred_element_type=F32
    ).astype(BF16)
    copies["sob"].wait()
    acc[...] += lax.dot_general(
        adapted, sob_buf[...], (((1,), (1,)), ((), ())), preferred_element_type=F32
    )
    stage_core(3)
    out_ref[...] = (acc[...] + base(3)).astype(out_ref.dtype)

    for c in range(len(payloads)):
        for copy in sends[c]:
            copy.wait_send()


def on_device(zs, ys, queries, key_cache, value_cache, lengths, ids, w, basis, sob, coef):
    n = zs * ys * 2
    reqs, ctx = key_cache.shape[:2]
    rank = basis.shape[1]
    wide = GROUP * HEAD_DIM
    smem = pl.BlockSpec(memory_space=pltpu.SMEM)
    hbm = pl.BlockSpec(memory_space=pl.ANY)
    vmem = pl.BlockSpec(memory_space=pltpu.VMEM)
    fetches = 5 + 2 * PAIRS
    return pl.pallas_call(
        functools.partial(kernel, zs, ys),
        out_shape=jax.ShapeDtypeStruct((n * reqs, w.shape[1]), BF16),
        in_specs=[smem, smem] + [hbm] * 7,
        out_specs=vmem,
        scratch_shapes=[
            pltpu.VMEM(queries.shape, BF16),
            pltpu.VMEM((PAIRS, reqs, ctx, 2 * HEAD_DIM), BF16),
            pltpu.VMEM((PAIRS, reqs, ctx, 2 * HEAD_DIM), BF16),
            pltpu.VMEM(w.shape, BF16),
            pltpu.VMEM(basis.shape, BF16),
            pltpu.VMEM(sob.shape, BF16),
            pltpu.VMEM(coef.shape, BF16),
            pltpu.VMEM((PAIRS, reqs, 2 * GROUP, 2 * HEAD_DIM), F32),
            pltpu.VMEM((PAIRS, reqs, 2 * GROUP, HEAD_DIM), F32),
            pltpu.VMEM((KV_HEADS, n, reqs, wide), BF16),
            pltpu.VMEM((n, reqs, rank), BF16),
            pltpu.VMEM((n, CAP, rank), BF16),
            pltpu.VMEM((n, reqs, HEAD_DIM), BF16),
            pltpu.VMEM((n * reqs, w.shape[1]), F32),
            pltpu.SemaphoreType.DMA((fetches,)),
            pltpu.SemaphoreType.DMA((KV_HEADS + 3, n)),
            pltpu.SemaphoreType.DMA((KV_HEADS + 3, n)),
        ],
        compiler_params=pltpu.CompilerParams(
            collective_id=0, has_side_effects=True, vmem_limit_bytes=58 * 1024 * 1024
        ),
    )(lengths, ids, queries, key_cache, value_cache, w, basis, sob, coef)


def solution(mesh):
    n = mesh.shape["adapter"]
    zs, ys = (4, 2) if n == 16 else (n // 2, 1)
    return jax.shard_map(
        functools.partial(on_device, zs, ys),
        mesh=mesh,
        in_specs=(
            P(("groups", "adapter"), None),
            P(("groups", "adapter"), None, None),
            P(("groups", "adapter"), None, None),
            P(("groups", "adapter")),
            P(("groups", "adapter")),
            P(None, "adapter"),
            P(),
            P("adapter", None),
            P("adapter", None, None),
        ),
        out_specs=P("groups", "adapter"),
        check_vma=False,
    )
```
